32 devices in a mesh: shell: 4 (over x, core), tile: 8 (over z, y).
Axes of the slice: x: 2, y: 2, z: 4, core: 2. Of those that a mesh axis runs over, the one named last changes fastest.
Arguments:
- residual: bfloat16 [16, 131072], P('shell', 'tile'), may hold values from -6 to 6
- tile_ray: int32 [1024], P('tile'), may hold values from 0 to 127, as said below
- filter_rows: bfloat16 [128, 128], replicated, may hold values from -0.5 to 0.5
- filter_cols: bfloat16 [128, 128], replicated, may hold values from -0.5 to 0.5
- band_lo: int32 [16], replicated, may hold values from 0 to 8
- shell_weight: float32 [16], replicated, may hold values from 0.3 to 3
Outputs:
- shell_grad: bfloat16 [16, 131072], P('shell', 'tile')
The draws below stay inside these ranges and needn't reach their ends.
Inputs may be any that keep to these rules, and one draw needn't show every extreme that they name: `tile_ray`: for each tile t, entries t * 128 to (t + 1) * 128 - 1 are a permutation of 0 to 127.
All inputs are finite; a program needn't handle non-finite values.
Results may differ from the reference program's by a relative error of at most 0.006.
Values may be sent and summed in bfloat16 or wider, within the bound.
A program may use at most 64 MiB of HBM per device.

```python
import math
import jax
import jax.numpy as jnp
from jax import lax

TILE_SIDE = 128
RAY_DEV = 16384
SHELLS = 16
BAND = 8
RAYS = 131072
N_TILE = 8


def draw_tile_ray(key, part):
    keys = jax.random.split(jax.random.fold_in(key, 11), N_TILE)
    orders = jax.vmap(lambda single: jax.random.permutation(single, TILE_SIDE))(keys)
    return orders.reshape(-1).astype(jnp.int32)


def place_ends(result, own_key, low, largest):
    extent = result.shape
    spot = [jax.random.randint(jax.random.fold_in(own_key, axis), (), 0, extent[axis]) for axis in range(len(extent))]
    result = result.at[tuple(spot)].set(low)
    longest = extent.index(max(extent))
    spot[longest] = (spot[longest] + 1) % extent[longest]
    return result.at[tuple(spot)].set(largest)


def steps_of(stream_key, dims, cuts, smallest, top_value):
    gain = 1.0
    for dim, blocks in cuts:
        steps = jax.random.uniform(jax.random.fold_in(jax.random.fold_in(stream_key, 6), dim), (blocks,), jnp.float32, smallest / len(cuts), top_value / len(cuts))
        gain = gain * jnp.repeat(jnp.exp(steps), dims[dim] // blocks).reshape((-1,) + (1,) * (len(dims) - 1 - dim))
    return gain


def gaussian(stream_key, extent, deviation, limit, shards=(), held_as=jnp.bfloat16):
    values = deviation * jax.random.normal(stream_key, extent, jnp.float32)
    if shards:
        values = values * steps_of(stream_key, extent, shards, -0.22, 0.18)
    return jnp.clip(values, -limit, limit).astype(held_as)


def setup_inputs(seed: int = 0) -> dict:
    streams_of = jax.random.split(jax.random.key(seed), 7)
    return {
        "residual": gaussian(streams_of[0], (SHELLS, RAYS), 1.0, 6.0, ((0, 4), (1, 8))),
        "tile_ray": draw_tile_ray(jax.random.fold_in(streams_of[6], 71), 0),
        "filter_rows": gaussian(streams_of[2], (TILE_SIDE, TILE_SIDE), TILE_SIDE ** -0.5, 0.5),
        "filter_cols": gaussian(streams_of[3], (TILE_SIDE, TILE_SIDE), TILE_SIDE ** -0.5, 0.5),
        "band_lo": place_ends(jax.random.randint(streams_of[4], (SHELLS,), 0, SHELLS - BAND + 1), jax.random.fold_in(streams_of[4], 1), 0, SHELLS - BAND).astype(jnp.int32),
        "shell_weight": jnp.clip(jnp.exp(jax.random.uniform(streams_of[5], (SHELLS,), jnp.float32, math.log(0.3), math.log(3.0))), 0.3, 3.0),
    }


def kernel_table(band_lo, shell_weight):
    count = shell_weight.shape[0]
    band = count // 2
    index = jnp.arange(count)
    chi_shell = (index.astype(jnp.float32) + 0.5) / count
    chi_source = (band_lo.astype(jnp.float32) + band) / count
    inside = (index[None, :] >= band_lo[:, None]) & (index[None, :] < band_lo[:, None] + band)
    values = 8.0 * shell_weight[None, :] * chi_shell[None, :] * (chi_source[:, None] - chi_shell[None, :]) / chi_source[:, None]
    return jnp.where(inside, values, jnp.zeros_like(values)).astype(jnp.bfloat16)


def reference(residual, tile_ray, filter_rows, filter_cols, band_lo, shell_weight):
    planes = residual.shape[0]
    ntile = N_TILE
    run = RAY_DEV // ntile
    side = filter_rows.shape[0]
    received = residual.reshape(planes, ntile, ntile, run).transpose(0, 2, 1, 3).reshape(planes, ntile, side, side)
    order = jnp.broadcast_to(tile_ray.reshape(1, ntile, side, 1), received.shape)
    pixels = jnp.take_along_axis(received, order, axis=2)
    image = pixels.astype(jnp.float32)
    half = jnp.einsum("stik,kb->stib", image, filter_cols.astype(jnp.float32), precision=lax.Precision.HIGHEST)
    whole = jnp.einsum("ia,stib->stab", filter_rows.astype(jnp.float32), half, precision=lax.Precision.HIGHEST)
    smoothed = whole.astype(jnp.bfloat16).reshape(planes, ntile * RAY_DEV)
    kernel = kernel_table(band_lo, shell_weight)
    return jnp.dot(kernel.T, smoothed, preferred_element_type=jnp.float32).astype(jnp.bfloat16)
```

```python
import functools

import jax
import jax.numpy as jnp
from jax import lax
from jax.experimental import pallas as pl
from jax.experimental.pallas import tpu as pltpu
from jax.sharding import PartitionSpec as P

MESH = pl.DeviceIdType.MESH
CORES = 2
F32 = jnp.float32
BF16 = jnp.bfloat16


def body(
    nshell, ntile, planes, group,
    rays, order, rows_in, cols_in, low_in, weight_in,
    out,
    recv, gath, half, acc, order_v, rows_v, cols_v, low_s, weight_s, table,
    local_sem, own_sem, a2a_send, a2a_recv, x_send, near_send, fwd_send, shell_recv,
):
    side = rows_v.shape[0]
    count = nshell * planes
    band = count // 2
    blk = rays.shape[0] // ntile
    nx = nshell // CORES
    sh, ti = lax.axis_index("shell"), lax.axis_index("tile")
    xi, core = sh // CORES, lax.rem(sh, CORES)
    partner = xi * CORES + (1 - core)

    def xpeer(e):
        return lax.rem(xi + e, nx) * CORES + core

    loads = [
        pltpu.make_async_copy(src, dst, local_sem.at[i])
        for i, (src, dst) in enumerate(
            [(order, order_v), (rows_in, rows_v), (cols_in, cols_v), (low_in, low_s), (weight_in, weight_s)]
        )
    ]

    barrier = pltpu.get_barrier_semaphore()

    def greet(e, _):
        pl.semaphore_signal(barrier, inc=1, device_id=(sh, lax.rem(ti + e, ntile)), device_id_type=MESH)
        return 0

    lax.fori_loop(1, ntile, greet, 0)
    pl.semaphore_signal(barrier, inc=1, device_id=(partner, ti), device_id_type=MESH)
    for e in range(1, nx):
        pl.semaphore_signal(barrier, inc=1, device_id=(xpeer(e), ti), device_id_type=MESH)

    for load in loads:
        load.start()
    own = pltpu.make_async_copy(rays.at[pl.ds(ti * blk, blk)], recv.at[pl.ds(ti * blk, blk)], own_sem)
    own.start()
    pl.semaphore_wait(barrier, ntile - 1 + nx)

    def block_to(e):
        to = lax.rem(ti + e, ntile)
        return pltpu.make_async_remote_copy(
            src_ref=rays.at[pl.ds(to * blk, blk)],
            dst_ref=recv.at[pl.ds(ti * blk, blk)],
            send_sem=a2a_send.at[e - 1],
            recv_sem=a2a_recv.at[e - 1],
            device_id=(sh, to),
            device_id_type=MESH,
        )

    def send(e, _):
        block_to(e).start()
        return 0

    lax.fori_loop(1, ntile, send, 0)

    for load in loads:
        load.wait()
    spot = lax.broadcasted_iota(jnp.int32, (side, side), 0)
    onehot = jnp.where(spot == order_v[...], 1.0, 0.0).astype(BF16)
    permuted = jnp.dot(onehot, rows_v[...], preferred_element_type=F32)
    filt = permuted.T.astype(BF16)
    cols = cols_v[...]

    which = lax.broadcasted_iota(jnp.int32, (count, side), 0)
    low = jnp.zeros((count, side), jnp.int32)
    for s in range(count):
        low = jnp.where(which == s, low_s[s], low)
    chi_source = (low.astype(F32) + band) / count
    for j in range(planes):
        shell = sh * planes + j
        chi_shell = (jnp.zeros((count, side), jnp.int32) + shell).astype(F32)
        chi_shell = (chi_shell + 0.5) / count
        value = 8.0 * weight_s[shell] * chi_shell * (chi_source - chi_shell) / chi_source
        value = jnp.where((low <= shell) & (shell < low + band), value, 0.0)
        table[j] = value.astype(BF16).astype(F32)

    step = blk * group
    own.wait()

    def column(e, _):
        @pl.when(e > 0)
        def _():
            block_to(jnp.maximum(e, 1)).wait_recv()

        source = lax.rem(ti - e + ntile, ntile)
        part = recv[pl.ds(source * blk, blk)]
        part = part.astype(F32).reshape(step, side).astype(BF16)
        half[pl.ds(pl.multiple_of(source * step, step), step), :] = jnp.dot(part, cols, preferred_element_type=F32)
        return 0

    lax.fori_loop(0, ntile, column, 0)

    def shell_copy(s, source, target, send_sem):
        return pltpu.make_async_remote_copy(
            src_ref=gath.at[source, s],
            dst_ref=gath.at[source, s],
            send_sem=send_sem,
            recv_sem=shell_recv.at[source, s],
            device_id=(target, ti),
            device_id_type=MESH,
        )

    for s in range(planes):
        plane = half[pl.ds(s, side, stride=planes), :].astype(BF16)
        gath[sh, s] = jnp.dot(filt, plane, preferred_element_type=F32).astype(BF16)
        for e in range(1, nx):
            shell_copy(s, sh, xpeer(e), x_send.at[e - 1, s]).start()
        shell_copy(s, sh, partner, near_send.at[s]).start()

    chunk = side // 4

    def mix(source, first):
        for c in range(0, side, chunk):
            got = [gath[source, s, pl.ds(c, chunk), :].astype(F32) for s in range(planes)]
            for j in range(planes):
                place = pl.ds(c * planes + j, chunk, stride=planes)
                total = None if first else acc[place, :]
                for s in range(planes):
                    term = table[j, pl.ds(source * planes + s, 1), :] * got[s]
                    total = term if total is None else total + term
                acc[place, :] = total

    mix(sh, True)
    for s in range(planes):
        shell_copy(s, partner, sh, near_send.at[s]).wait_recv()
    mix(partner, False)
    for e in range(1, nx):
        source = xpeer(nx - e)
        for s in range(planes):
            shell_copy(s, source, sh, x_send.at[e - 1, s]).wait_recv()
            shell_copy(s, source, partner, fwd_send.at[e - 1, s]).start()
        mix(source, False)
    for e in range(1, nx):
        source = lax.rem(xi + nx - e, nx) * CORES + (1 - core)
        for s in range(planes):
            shell_copy(s, source, sh, fwd_send.at[e - 1, s]).wait_recv()
        mix(source, False)
    out[...] = acc[...].astype(BF16).reshape(out.shape)

    def sent(e, _):
        block_to(e).wait_send()
        return 0

    lax.fori_loop(1, ntile, sent, 0)
    for s in range(planes):
        shell_copy(s, sh, partner, near_send.at[s]).wait_send()
        for e in range(1, nx):
            shell_copy(s, sh, xpeer(e), x_send.at[e - 1, s]).wait_send()
            shell_copy(s, xpeer(nx - e), partner, fwd_send.at[e - 1, s]).wait_send()


def shards(residual, tile_ray, filter_rows, filter_cols, band_lo, shell_weight):
    planes, rays = residual.shape
    nshell, ntile = lax.axis_size("shell"), lax.axis_size("tile")
    side = filter_rows.shape[0]
    count = band_lo.shape[0]
    nx = nshell // CORES
    per = side // ntile
    fold = 4 if per % 4 == 0 else 1
    group = planes * fold
    major = side // fold
    arranged = residual.reshape(planes, side, side).transpose(1, 0, 2).reshape(major, group, side)
    dma = pltpu.SemaphoreType.DMA
    result = pl.pallas_call(
        functools.partial(body, nshell, ntile, planes, group),
        out_shape=jax.ShapeDtypeStruct((major, group, side), BF16),
        in_specs=[pl.BlockSpec(memory_space=pl.ANY)] * 6,
        out_specs=pl.BlockSpec(memory_space=pltpu.VMEM),
        scratch_shapes=[
            pltpu.VMEM((major, group, side), BF16),
            pltpu.VMEM((nshell, planes, side, side), BF16),
            pltpu.VMEM((side * planes, side), F32),
            pltpu.VMEM((side * planes, side), F32),
            pltpu.VMEM((1, side), jnp.int32),
            pltpu.VMEM((side, side), BF16),
            pltpu.VMEM((side, side), BF16),
            pltpu.SMEM((count,), jnp.int32),
            pltpu.SMEM((count,), F32),
            pltpu.VMEM((planes, count, side), F32),
            dma((5,)),
            dma,
            dma((ntile - 1,)),
            dma((ntile - 1,)),
            dma((nx - 1, planes)),
            dma((planes,)),
            dma((nx - 1, planes)),
            dma((nshell, planes)),
        ],
        compiler_params=pltpu.CompilerParams(
            collective_id=0, has_side_effects=True, vmem_limit_bytes=32 * 1024 * 1024
        ),
    )(arranged, tile_ray.reshape(1, side), filter_rows, filter_cols, band_lo, shell_weight)
    return result.reshape(side, planes, side).transpose(1, 0, 2).reshape(planes, rays)


def solution(mesh):
    in_specs = (P("shell", "tile"), P("tile"), P(), P(), P(), P())
    out_specs = P("shell", "tile")
    return jax.shard_map(shards, mesh=mesh, in_specs=in_specs, out_specs=out_specs, check_vma=False)
```

```python
import functools

import jax
import jax.numpy as jnp
from jax import lax
from jax.experimental import pallas as pl
from jax.experimental.pallas import tpu as pltpu
from jax.sharding import PartitionSpec as P

MESH = pl.DeviceIdType.MESH
CORES = 2
F32 = jnp.float32
BF16 = jnp.bfloat16


def body(
    nshell, ntile, planes,
    rays, order, rows_in, cols_in, low_in, weight_in,
    out,
    stage, leave, recv, gath, half, acc, order_v, rows_v, cols_v, low_s, weight_s, table,
    local_sem, a2a_send, a2a_recv, x_send, near_send, fwd_send, shell_recv,
):
    side = rows_v.shape[0]
    count = nshell * planes
    band = count // 2
    blk = side // ntile
    nx = nshell // CORES
    sh, ti = lax.axis_index("shell"), lax.axis_index("tile")
    xi, core = sh // CORES, lax.rem(sh, CORES)
    partner = xi * CORES + (1 - core)

    def xpeer(e):
        return lax.rem(xi + e, nx) * CORES + core

    barrier = pltpu.get_barrier_semaphore()

    def greet(e, _):
        pl.semaphore_signal(barrier, inc=1, device_id=(sh, lax.rem(ti + e, ntile)), device_id_type=MESH)
        return 0

    lax.fori_loop(1, ntile, greet, 0, unroll=ntile <= 8)
    pl.semaphore_signal(barrier, inc=1, device_id=(partner, ti), device_id_type=MESH)
    for e in range(1, nx):
        pl.semaphore_signal(barrier, inc=1, device_id=(xpeer(e), ti), device_id_type=MESH)

    pairs = [
        (rays, stage), (cols_in, cols_v), (order, order_v), (rows_in, rows_v), (low_in, low_s), (weight_in, weight_s)
    ]
    loads = [pltpu.make_async_copy(src, dst, local_sem.at[i]) for i, (src, dst) in enumerate(pairs)]
    for load in loads:
        load.start()

    loads[0].wait()
    loads[1].wait()
    mine = stage[...]
    if mine.shape[1] % 16:
        mine = mine.astype(F32).reshape(half.shape).astype(BF16)
    half[...] = jnp.dot(mine.reshape(half.shape), cols_v[...], preferred_element_type=F32)
    for s in range(planes):
        leave[s] = half[pl.ds(s, side, stride=planes), :].reshape(ntile, blk, side).astype(BF16)

    pl.semaphore_wait(barrier, ntile - 1 + nx)

    for s in range(planes):

        def send(e, _):
            to = lax.rem(ti + e, ntile)
            pltpu.make_async_remote_copy(
                src_ref=leave.at[s, to],
                dst_ref=recv.at[s, ti],
                send_sem=a2a_send,
                recv_sem=a2a_recv.at[s],
                device_id=(sh, to),
                device_id_type=MESH,
            ).start()
            return 0

        lax.fori_loop(1, ntile, send, 0, unroll=ntile <= 8)
    for s in range(planes):
        recv[s, ti] = leave[s, ti]

    for load in loads[2:]:
        load.wait()
    spot = lax.broadcasted_iota(jnp.int32, (side, side), 0)
    onehot = jnp.where(spot == order_v[...], 1.0, 0.0).astype(BF16)
    permuted = jnp.dot(onehot, rows_v[...], preferred_element_type=F32)
    filt = permuted.T.astype(BF16)

    which = lax.broadcasted_iota(jnp.int32, (count, side), 0)
    low = jnp.zeros((count, side), jnp.int32)
    for s in range(count):
        low = jnp.where(which == s, low_s[s], low)
    chi_source = (low.astype(F32) + band) / count
    for j in range(planes):
        shell = sh * planes + j
        chi_shell = (jnp.zeros((count, side), jnp.int32) + shell).astype(F32)
        chi_shell = (chi_shell + 0.5) / count
        value = 8.0 * weight_s[shell] * chi_shell * (chi_source - chi_shell) / chi_source
        value = jnp.where((low <= shell) & (shell < low + band), value, 0.0)
        table[j] = value.astype(BF16).astype(F32)

    def shell_copy(s, source, target, send_sem):
        return pltpu.make_async_remote_copy(
            src_ref=gath.at[source, s],
            dst_ref=gath.at[source, s],
            send_sem=send_sem,
            recv_sem=shell_recv.at[source, s],
            device_id=(target, ti),
            device_id_type=MESH,
        )

    def forward(s):
        for e in range(1, nx):
            source = xpeer(nx - e)
            shell_copy(s, source, sh, x_send.at[e - 1, s]).wait_recv()
            shell_copy(s, source, partner, fwd_send.at[e - 1, s]).start()

    chunk = side // 4

    def mix(source, those, first=False, last=False):
        for c in range(0, side, chunk):
            got = [gath[source, s, pl.ds(c, chunk), :].astype(F32) for s in those]
            for j in range(planes):
                total = None if first else acc[j, pl.ds(c, chunk), :]
                for s, plane in zip(those, got):
                    term = table[j, pl.ds(source * planes + s, 1), :] * plane
                    total = term if total is None else total + term
                if last:
                    half[pl.ds(c * planes + j, chunk, stride=planes), :] = total
                else:
                    acc[j, pl.ds(c, chunk), :] = total

    for s in range(planes):
        landed = recv.at[s, pl.ds(0, ntile - 1)]
        pltpu.make_async_copy(landed, landed, a2a_recv.at[s]).wait()
        plane = recv[s]
        if blk % 16:
            plane = plane.astype(F32).reshape(side, side).astype(BF16)
        gath[sh, s] = jnp.dot(filt, plane.reshape(side, side), preferred_element_type=F32).astype(BF16)
        for e in range(1, nx):
            shell_copy(s, sh, xpeer(e), x_send.at[e - 1, s]).start()
        shell_copy(s, sh, partner, near_send.at[s]).start()
        mix(sh, [s], first=s == 0)
        if s >= 2:
            forward(s - 2)

    for s in range(max(planes - 2, 0), planes):
        forward(s)
        if s < planes - 1:
            for t in range(planes):
                shell_copy(t, partner, sh, near_send.at[t]).wait_recv()
            mix(partner, list(range(planes)))
    for e in range(1, nx):
        mix(xpeer(nx - e), list(range(planes)))
    for e in range(1, nx):
        source = lax.rem(xi + nx - e, nx) * CORES + (1 - core)
        for s in range(planes):
            shell_copy(s, source, sh, fwd_send.at[e - 1, s]).wait_recv()
            mix(source, [s], last=e == nx - 1 and s == planes - 1)
    out[...] = half[...].astype(BF16).reshape(out.shape)

    gone = leave.at[pl.ds(0, planes), pl.ds(0, ntile - 1)]
    pltpu.make_async_copy(gone, gone, a2a_send).wait()
    for s in range(planes):
        shell_copy(s, sh, partner, near_send.at[s]).wait_send()
        for e in range(1, nx):
            shell_copy(s, sh, xpeer(e), x_send.at[e - 1, s]).wait_send()
            shell_copy(s, xpeer(nx - e), partner, fwd_send.at[e - 1, s]).wait_send()


def shards(residual, tile_ray, filter_rows, filter_cols, band_lo, shell_weight):
    planes, rays = residual.shape
    nshell, ntile = lax.axis_size("shell"), lax.axis_size("tile")
    side = filter_rows.shape[0]
    count = band_lo.shape[0]
    nx = nshell // CORES
    blk = side // ntile
    fold = 4 if side % 4 == 0 else 1
    major, group = side // fold, planes * fold
    arranged = residual.reshape(planes, side, side).transpose(1, 0, 2).reshape(major, group, side)
    operands = (arranged, tile_ray.reshape(1, side), filter_rows, filter_cols, band_lo, shell_weight)
    dma = pltpu.SemaphoreType.DMA
    result = pl.pallas_call(
        functools.partial(body, nshell, ntile, planes),
        out_shape=jax.ShapeDtypeStruct((major, group, side), BF16),
        in_specs=[pl.BlockSpec(memory_space=pltpu.HBM)] * 6,
        out_specs=pl.BlockSpec(memory_space=pltpu.VMEM),
        scratch_shapes=[
            pltpu.VMEM((major, group, side), BF16),
            pltpu.VMEM((planes, ntile, blk, side), BF16),
            pltpu.VMEM((planes, ntile, blk, side), BF16),
            pltpu.VMEM((nshell, planes, side, side), BF16),
            pltpu.VMEM((side * planes, side), F32),
            pltpu.VMEM((planes, side, side), F32),
            pltpu.VMEM((1, side), jnp.int32),
            pltpu.VMEM((side, side), BF16),
            pltpu.VMEM((side, side), BF16),
            pltpu.SMEM((count,), jnp.int32),
            pltpu.SMEM((count,), F32),
            pltpu.VMEM((planes, count, side), F32),
            dma((6,)),
            dma,
            dma((planes,)),
            dma((nx - 1, planes)),
            dma((planes,)),
            dma((nx - 1, planes)),
            dma((nshell, planes)),
        ],
        compiler_params=pltpu.CompilerParams(
            collective_id=0, has_side_effects=True, vmem_limit_bytes=16 * 1024 * 1024
        ),
    )(*(pltpu.with_memory_space_constraint(x, pltpu.HBM) for x in operands))
    return result.reshape(side, planes, side).transpose(1, 0, 2).reshape(planes, rays)


def solution(mesh):
    in_specs = (P("shell", "tile"), P("tile"), P(), P(), P(), P())
    out_specs = P("shell", "tile")
    return jax.shard_map(shards, mesh=mesh, in_specs=in_specs, out_specs=out_specs, check_vma=False)
```

```python
import functools

import jax
import jax.numpy as jnp
from jax import lax
from jax.experimental import pallas as pl
from jax.experimental.pallas import tpu as pltpu
from jax.sharding import PartitionSpec as P

MESH = pl.DeviceIdType.MESH
CORES = 2
PARTS = 2
F32 = jnp.float32
BF16 = jnp.bfloat16


def body(
    nshell, ntile, planes,
    rays, order, rows_in, cols_in, low_in, weight_in,
    out,
    stage, leave, recv, gath, half, acc, order_v, rows_v, cols_v, low_s, weight_s, table,
    local_sem, a2a_send, a2a_recv, x_send, near_send, fwd_send, shell_recv,
):
    side = rows_v.shape[0]
    count = nshell * planes
    band = count // 2
    blk = side // ntile
    nx = nshell // CORES
    sh, ti = lax.axis_index("shell"), lax.axis_index("tile")
    xi, core = sh // CORES, lax.rem(sh, CORES)
    partner = xi * CORES + (1 - core)

    def xpeer(e):
        return lax.rem(xi + e, nx) * CORES + core

    barrier = pltpu.get_barrier_semaphore()

    def greet(e, _):
        pl.semaphore_signal(barrier, inc=1, device_id=(sh, lax.rem(ti + e, ntile)), device_id_type=MESH)
        return 0

    lax.fori_loop(1, ntile, greet, 0, unroll=ntile <= 8)
    pl.semaphore_signal(barrier, inc=1, device_id=(partner, ti), device_id_type=MESH)
    for e in range(1, nx):
        pl.semaphore_signal(barrier, inc=1, device_id=(xpeer(e), ti), device_id_type=MESH)

    pairs = [
        (rays, stage), (cols_in, cols_v), (order, order_v), (rows_in, rows_v), (low_in, low_s), (weight_in, weight_s)
    ]
    loads = [pltpu.make_async_copy(src, dst, local_sem.at[i]) for i, (src, dst) in enumerate(pairs)]
    for load in loads:
        load.start()

    loads[0].wait()
    loads[1].wait()
    mine = stage[...]
    if mine.shape[1] % 16:
        mine = mine.astype(F32).reshape(half.shape).astype(BF16)
    half[...] = jnp.dot(mine.reshape(half.shape), cols_v[...], preferred_element_type=F32)
    parts, _, per = leave.shape[:3]
    for h in range(parts):
        for p in range(per):
            plane = half[pl.ds(h * per + p, side, stride=planes), :]
            leave[h, :, p] = plane.reshape(ntile, blk, side).astype(BF16)
        if h == 0:
            pl.semaphore_wait(barrier, ntile - 1 + nx)

        def send(e, _):
            to = lax.rem(ti + e, ntile)
            pltpu.make_async_remote_copy(
                src_ref=leave.at[h, to],
                dst_ref=recv.at[h, ti],
                send_sem=a2a_send,
                recv_sem=a2a_recv.at[h],
                device_id=(sh, to),
                device_id_type=MESH,
            ).start()
            return 0

        lax.fori_loop(1, ntile, send, 0, unroll=ntile <= 8)
    for h in range(parts):
        recv[h, ti] = leave[h, ti]

    for load in loads[2:]:
        load.wait()
    spot = lax.broadcasted_iota(jnp.int32, (side, side), 0)
    onehot = jnp.where(spot == order_v[...], 1.0, 0.0).astype(BF16)
    permuted = jnp.dot(onehot, rows_v[...], preferred_element_type=F32)
    filt = permuted.T.astype(BF16)

    which = lax.broadcasted_iota(jnp.int32, (count, side), 0)
    low = jnp.zeros((count, side), jnp.int32)
    for s in range(count):
        low = jnp.where(which == s, low_s[s], low)
    chi_source = (low.astype(F32) + band) / count
    for j in range(planes):
        shell = sh * planes + j
        chi_shell = (jnp.zeros((count, side), jnp.int32) + shell).astype(F32)
        chi_shell = (chi_shell + 0.5) / count
        value = 8.0 * weight_s[shell] * chi_shell * (chi_source - chi_shell) / chi_source
        value = jnp.where((low <= shell) & (shell < low + band), value, 0.0)
        table[j] = value.astype(BF16).astype(F32)

    def shell_copy(s, source, target, send_sem):
        return pltpu.make_async_remote_copy(
            src_ref=gath.at[source, s],
            dst_ref=gath.at[source, s],
            send_sem=send_sem,
            recv_sem=shell_recv.at[source, s],
            device_id=(target, ti),
            device_id_type=MESH,
        )

    def forward(s):
        for e in range(1, nx):
            source = xpeer(nx - e)
            shell_copy(s, source, sh, x_send.at[e - 1, s]).wait_recv()
            shell_copy(s, source, partner, fwd_send.at[e - 1, s]).start()

    chunk = side // 4

    def mix(source, those, first=False, last=False):
        def rows(i, _):
            c = i * chunk if last else pl.multiple_of(i * chunk, chunk)
            got = [gath[source, s, pl.ds(c, chunk), :].astype(F32) for s in those]
            for j in range(planes):
                total = None if first else acc[j, pl.ds(c, chunk), :]
                for s, plane in zip(those, got):
                    term = table[j, pl.ds(source * planes + s, 1), :] * plane
                    total = term if total is None else total + term
                if last:
                    half[pl.ds(c * planes + j, chunk, stride=planes), :] = total
                else:
                    acc[j, pl.ds(c, chunk), :] = total
            return 0

        if last:
            for i in range(side // chunk):
                rows(i, 0)
        else:
            lax.fori_loop(0, side // chunk, rows, 0)

    for s in range(planes):
        h, p = s // per, s % per
        if p == 0:
            landed = recv.at[h, pl.ds(0, ntile - 1)]
            pltpu.make_async_copy(landed, landed, a2a_recv.at[h]).wait()
        plane = recv[h, :, p]
        if blk % 16:
            plane = plane.astype(F32).reshape(side, side).astype(BF16)
        gath[sh, s] = jnp.dot(filt, plane.reshape(side, side), preferred_element_type=F32).astype(BF16)
        for e in range(1, nx):
            shell_copy(s, sh, xpeer(e), x_send.at[e - 1, s]).start()
        shell_copy(s, sh, partner, near_send.at[s]).start()
        mix(sh, [s], first=s == 0)
        if s >= 2:
            forward(s - 2)

    for s in range(max(planes - 2, 0), planes):
        forward(s)
        if s < planes - 1:
            for t in range(planes):
                shell_copy(t, partner, sh, near_send.at[t]).wait_recv()
            mix(partner, list(range(planes)))
    for e in range(1, nx):
        mix(xpeer(nx - e), list(range(planes)))
    for e in range(1, nx):
        source = lax.rem(xi + nx - e, nx) * CORES + (1 - core)
        for s in range(planes):
            shell_copy(s, source, sh, fwd_send.at[e - 1, s]).wait_recv()
            mix(source, [s], last=e == nx - 1 and s == planes - 1)
    out[...] = half[...].astype(BF16).reshape(out.shape)

    gone = leave.at[pl.ds(0, parts), pl.ds(0, ntile - 1)]
    pltpu.make_async_copy(gone, gone, a2a_send).wait()
    for s in range(planes):
        shell_copy(s, sh, partner, near_send.at[s]).wait_send()
        for e in range(1, nx):
            shell_copy(s, sh, xpeer(e), x_send.at[e - 1, s]).wait_send()
            shell_copy(s, xpeer(nx - e), partner, fwd_send.at[e - 1, s]).wait_send()


def shards(residual, tile_ray, filter_rows, filter_cols, band_lo, shell_weight):
    planes, rays = residual.shape
    nshell, ntile = lax.axis_size("shell"), lax.axis_size("tile")
    side = filter_rows.shape[0]
    count = band_lo.shape[0]
    nx = nshell // CORES
    blk = side // ntile
    fold = 4 if side % 4 == 0 else 1
    major, group = side // fold, planes * fold
    arranged = residual.reshape(planes, side, side).transpose(1, 0, 2).reshape(major, group, side)
    operands = (arranged, tile_ray.reshape(1, side), filter_rows, filter_cols, band_lo, shell_weight)
    dma = pltpu.SemaphoreType.DMA
    result = pl.pallas_call(
        functools.partial(body, nshell, ntile, planes),
        out_shape=jax.ShapeDtypeStruct((major, group, side), BF16),
        in_specs=[pl.BlockSpec(memory_space=pltpu.HBM)] * 6,
        out_specs=pl.BlockSpec(memory_space=pltpu.VMEM),
        scratch_shapes=[
            pltpu.VMEM((major, group, side), BF16),
            pltpu.VMEM((PARTS, ntile, planes // PARTS, blk, side), BF16),
            pltpu.VMEM((PARTS, ntile, planes // PARTS, blk, side), BF16),
            pltpu.VMEM((nshell, planes, side, side), BF16),
            pltpu.VMEM((side * planes, side), F32),
            pltpu.VMEM((planes, side, side), F32),
            pltpu.VMEM((1, side), jnp.int32),
            pltpu.VMEM((side, side), BF16),
            pltpu.VMEM((side, side), BF16),
            pltpu.SMEM((count,), jnp.int32),
            pltpu.SMEM((count,), F32),
            pltpu.VMEM((planes, count, side), F32),
            dma((6,)),
            dma,
            dma((PARTS,)),
            dma((nx - 1, planes)),
            dma((planes,)),
            dma((nx - 1, planes)),
            dma((nshell, planes)),
        ],
        compiler_params=pltpu.CompilerParams(
            collective_id=0, has_side_effects=True, vmem_limit_bytes=16 * 1024 * 1024
        ),
    )(*(pltpu.with_memory_space_constraint(x, pltpu.HBM) for x in operands))
    return result.reshape(side, planes, side).transpose(1, 0, 2).reshape(planes, rays)


def solution(mesh):
    in_specs = (P("shell", "tile"), P("tile"), P(), P(), P(), P())
    out_specs = P("shell", "tile")
    return jax.shard_map(shards, mesh=mesh, in_specs=in_specs, out_specs=out_specs, check_vma=False)
```

```python
import functools

import jax
import jax.numpy as jnp
from jax import lax
from jax.experimental import pallas as pl
from jax.experimental.pallas import tpu as pltpu
from jax.sharding import PartitionSpec as P

MESH = pl.DeviceIdType.MESH
CORES = 2
F32 = jnp.float32
BF16 = jnp.bfloat16


def body(
    nshell, ntile, planes,
    rays, order, rows_in, cols_in, low_in, weight_in,
    out,
    stage, gath, half, acc, order_v, rows_v, cols_v, low_s, weight_s, table,
    local_sem, a2a_send, a2a_recv, x_send, near_send, fwd_send, shell_recv,
):
    side = rows_v.shape[0]
    count = nshell * planes
    band = count // 2
    nx = nshell // CORES
    sh, ti = lax.axis_index("shell"), lax.axis_index("tile")
    xi, core = sh // CORES, lax.rem(sh, CORES)
    partner = xi * CORES + (1 - core)

    def xpeer(e):
        return lax.rem(xi + e, nx) * CORES + core

    barrier = pltpu.get_barrier_semaphore()

    def greet(e, _):
        pl.semaphore_signal(barrier, inc=1, device_id=(sh, lax.rem(ti + e, ntile)), device_id_type=MESH)
        return 0

    lax.fori_loop(1, ntile, greet, 0, unroll=ntile <= 8)
    pl.semaphore_signal(barrier, inc=1, device_id=(partner, ti), device_id_type=MESH)
    for e in range(1, nx):
        pl.semaphore_signal(barrier, inc=1, device_id=(xpeer(e), ti), device_id_type=MESH)

    lead = rays.shape[0] // ntile
    own = pl.ds(ti * lead, lead)
    pairs = [
        (rays.at[own], stage.at[own]), (order, order_v), (rows_in, rows_v), (cols_in, cols_v), (low_in, low_s), (weight_in, weight_s)
    ]
    loads = [pltpu.make_async_copy(src, dst, local_sem.at[i]) for i, (src, dst) in enumerate(pairs)]
    for load in loads:
        load.start()
    pl.semaphore_wait(barrier, ntile - 1 + nx)

    def send(e, _):
        to = lax.rem(ti + e, ntile)
        pltpu.make_async_remote_copy(
            src_ref=rays.at[pl.ds(to * lead, lead)],
            dst_ref=stage.at[own],
            send_sem=a2a_send,
            recv_sem=a2a_recv,
            device_id=(sh, to),
            device_id_type=MESH,
        ).start()
        return 0

    lax.fori_loop(1, ntile, send, 0, unroll=ntile <= 8)

    for load in loads:
        load.wait()
    spot = lax.broadcasted_iota(jnp.int32, (side, side), 0)
    onehot = jnp.where(spot == order_v[...], 1.0, 0.0).astype(BF16)
    permuted = jnp.dot(onehot, rows_v[...], preferred_element_type=F32)
    filt = permuted.T.astype(BF16)

    which = lax.broadcasted_iota(jnp.int32, (count, side), 0)
    low = jnp.zeros((count, side), jnp.int32)
    for s in range(count):
        low = jnp.where(which == s, low_s[s], low)
    chi_source = (low.astype(F32) + band) / count
    for j in range(planes):
        shell = sh * planes + j
        chi_shell = (jnp.zeros((count, side), jnp.int32) + shell).astype(F32)
        chi_shell = (chi_shell + 0.5) / count
        value = 8.0 * weight_s[shell] * chi_shell * (chi_source - chi_shell) / chi_source
        value = jnp.where((low <= shell) & (shell < low + band), value, 0.0)
        table[j] = value.astype(BF16).astype(F32)

    def shell_copy(s, source, target, send_sem):
        return pltpu.make_async_remote_copy(
            src_ref=gath.at[source, s],
            dst_ref=gath.at[source, s],
            send_sem=send_sem,
            recv_sem=shell_recv.at[source, s],
            device_id=(target, ti),
            device_id_type=MESH,
        )

    def forward(s):
        for e in range(1, nx):
            source = xpeer(nx - e)
            shell_copy(s, source, sh, x_send.at[e - 1, s]).wait_recv()
            shell_copy(s, source, partner, fwd_send.at[e - 1, s]).start()

    chunk = side // 4

    def mix(source, those, first=False, last=False):
        def rows(i, _):
            c = i * chunk if last else pl.multiple_of(i * chunk, chunk)
            got = [gath[source, s, pl.ds(c, chunk), :].astype(F32) for s in those]
            for j in range(planes):
                total = None if first else acc[j, pl.ds(c, chunk), :]
                for s, plane in zip(those, got):
                    term = table[j, pl.ds(source * planes + s, 1), :] * plane
                    total = term if total is None else total + term
                if last:
                    half[pl.ds(c * planes + j, chunk, stride=planes), :] = total
                else:
                    acc[j, pl.ds(c, chunk), :] = total
            return 0

        if last:
            for i in range(side // chunk):
                rows(i, 0)
        else:
            lax.fori_loop(0, side // chunk, rows, 0)

    landed = stage.at[pl.ds(0, (ntile - 1) * lead)]
    pltpu.make_async_copy(landed, landed, a2a_recv).wait()
    pixels = stage[...]
    if pixels.shape[1] % 16:
        pixels = pixels.astype(F32).reshape(half.shape).astype(BF16)
    half[...] = jnp.dot(pixels.reshape(half.shape), cols_v[...], preferred_element_type=F32)
    for s in range(planes):
        plane = half[pl.ds(s, side, stride=planes), :].astype(BF16)
        gath[sh, s] = jnp.dot(filt, plane, preferred_element_type=F32).astype(BF16)
        for e in range(1, nx):
            shell_copy(s, sh, xpeer(e), x_send.at[e - 1, s]).start()
        shell_copy(s, sh, partner, near_send.at[s]).start()
    mix(sh, list(range(planes)), first=True)
    for s in range(planes):
        forward(s)
        if s == 0:
            for t in range(planes):
                shell_copy(t, partner, sh, near_send.at[t]).wait_recv()
            mix(partner, list(range(planes)))
    for e in range(1, nx):
        mix(xpeer(nx - e), list(range(planes)))
    for e in range(1, nx):
        source = lax.rem(xi + nx - e, nx) * CORES + (1 - core)
        for s in range(planes):
            shell_copy(s, source, sh, fwd_send.at[e - 1, s]).wait_recv()
            mix(source, [s], last=e == nx - 1 and s == planes - 1)
    out[...] = half[...].astype(BF16).reshape(out.shape)

    gone = rays.at[pl.ds(0, (ntile - 1) * lead)]
    pltpu.make_async_copy(gone, gone, a2a_send).wait()
    for s in range(planes):
        shell_copy(s, sh, partner, near_send.at[s]).wait_send()
        for e in range(1, nx):
            shell_copy(s, sh, xpeer(e), x_send.at[e - 1, s]).wait_send()
            shell_copy(s, xpeer(nx - e), partner, fwd_send.at[e - 1, s]).wait_send()


def shards(residual, tile_ray, filter_rows, filter_cols, band_lo, shell_weight):
    planes, rays = residual.shape
    nshell, ntile = lax.axis_size("shell"), lax.axis_size("tile")
    side = filter_rows.shape[0]
    count = band_lo.shape[0]
    nx = nshell // CORES
    blk = side // ntile
    fold = 4 if blk % 4 == 0 else 1
    major, group = side // fold, planes * fold
    arranged = residual.reshape(planes, side, side).transpose(1, 0, 2).reshape(major, group, side)
    operands = (arranged, tile_ray.reshape(1, side), filter_rows, filter_cols, band_lo, shell_weight)
    dma = pltpu.SemaphoreType.DMA
    result = pl.pallas_call(
        functools.partial(body, nshell, ntile, planes),
        out_shape=jax.ShapeDtypeStruct((major, group, side), BF16),
        in_specs=[pl.BlockSpec(memory_space=pltpu.HBM)] * 6,
        out_specs=pl.BlockSpec(memory_space=pltpu.VMEM),
        scratch_shapes=[
            pltpu.VMEM((major, group, side), BF16),
            pltpu.VMEM((nshell, planes, side, side), BF16),
            pltpu.VMEM((side * planes, side), F32),
            pltpu.VMEM((planes, side, side), F32),
            pltpu.VMEM((1, side), jnp.int32),
            pltpu.VMEM((side, side), BF16),
            pltpu.VMEM((side, side), BF16),
            pltpu.SMEM((count,), jnp.int32),
            pltpu.SMEM((count,), F32),
            pltpu.VMEM((planes, count, side), F32),
            dma((6,)),
            dma,
            dma,
            dma((nx - 1, planes)),
            dma((planes,)),
            dma((nx - 1, planes)),
            dma((nshell, planes)),
        ],
        compiler_params=pltpu.CompilerParams(
            collective_id=0, has_side_effects=True, vmem_limit_bytes=16 * 1024 * 1024
        ),
    )(*(pltpu.with_memory_space_constraint(x, pltpu.HBM) for x in operands))
    return result.reshape(side, planes, side).transpose(1, 0, 2).reshape(planes, rays)


def solution(mesh):
    in_specs = (P("shell", "tile"), P("tile"), P(), P(), P(), P())
    out_specs = P("shell", "tile")
    return jax.shard_map(shards, mesh=mesh, in_specs=in_specs, out_specs=out_specs, check_vma=False)
```

```python
import functools

import jax
import jax.numpy as jnp
from jax import lax
from jax.experimental import pallas as pl
from jax.experimental.pallas import tpu as pltpu
from jax.sharding import PartitionSpec as P

MESH = pl.DeviceIdType.MESH
CORES = 2
F32 = jnp.float32
BF16 = jnp.bfloat16


def body(
    nshell, ntile, planes,
    rays, order, rows_in, cols_in, low_in, weight_in,
    out,
    stage, gath, half, acc, order_v, rows_v, cols_v, low_s, weight_s, table,
    local_sem, a2a_send, a2a_recv, x_send, near_send, fwd_send, shell_recv,
):
    side = rows_v.shape[0]
    count = nshell * planes
    band = count // 2
    nx = nshell // CORES
    sh, ti = lax.axis_index("shell"), lax.axis_index("tile")
    xi, core = sh // CORES, lax.rem(sh, CORES)
    partner = xi * CORES + (1 - core)

    def xpeer(e):
        return lax.rem(xi + e, nx) * CORES + core

    barrier = pltpu.get_barrier_semaphore()

    def greet(e, _):
        pl.semaphore_signal(barrier, inc=1, device_id=(sh, lax.rem(ti + e, ntile)), device_id_type=MESH)
        return 0

    lax.fori_loop(1, ntile, greet, 0, unroll=ntile <= 8)
    pl.semaphore_signal(barrier, inc=1, device_id=(partner, ti), device_id_type=MESH)
    for e in range(1, nx):
        pl.semaphore_signal(barrier, inc=1, device_id=(xpeer(e), ti), device_id_type=MESH)

    lead = rays.shape[0] // ntile
    own = pl.ds(ti * lead, lead)
    pairs = [
        (rays.at[own], stage.at[own]), (order, order_v), (rows_in, rows_v), (cols_in, cols_v), (low_in, low_s), (weight_in, weight_s)
    ]
    loads = [pltpu.make_async_copy(src, dst, local_sem.at[i]) for i, (src, dst) in enumerate(pairs)]
    for load in loads:
        load.start()
    pl.semaphore_wait(barrier, ntile - 1 + nx)

    def send(e, _):
        to = lax.rem(ti + e, ntile)
        pltpu.make_async_remote_copy(
            src_ref=rays.at[pl.ds(to * lead, lead)],
            dst_ref=stage.at[own],
            send_sem=a2a_send,
            recv_sem=a2a_recv,
            device_id=(sh, to),
            device_id_type=MESH,
        ).start()
        return 0

    lax.fori_loop(1, ntile, send, 0, unroll=ntile <= 8)

    for load in loads:
        load.wait()
    spot = lax.broadcasted_iota(jnp.int32, (side, side), 0)
    onehot = jnp.where(spot == order_v[...], 1.0, 0.0).astype(BF16)
    permuted = jnp.dot(onehot, rows_v[...], preferred_element_type=F32)
    filt = permuted.T.astype(BF16)

    which = lax.broadcasted_iota(jnp.int32, (count, side), 0)
    low = jnp.zeros((count, side), jnp.int32)
    for s in range(count):
        low = jnp.where(which == s, low_s[s], low)
    chi_source = (low.astype(F32) + band) / count
    for j in range(planes):
        shell = sh * planes + j
        chi_shell = (jnp.zeros((count, side), jnp.int32) + shell).astype(F32)
        chi_shell = (chi_shell + 0.5) / count
        value = 8.0 * weight_s[shell] * chi_shell * (chi_source - chi_shell) / chi_source
        value = jnp.where((low <= shell) & (shell < low + band), value, 0.0)
        table[j] = value.astype(BF16).astype(F32)

    def shell_copy(s, source, target, send_sem):
        return pltpu.make_async_remote_copy(
            src_ref=gath.at[source, s],
            dst_ref=gath.at[source, s],
            send_sem=send_sem,
            recv_sem=shell_recv.at[source, s],
            device_id=(target, ti),
            device_id_type=MESH,
        )

    def forward(s):
        for e in range(1, nx):
            source = xpeer(nx - e)
            shell_copy(s, source, sh, x_send.at[e - 1, s]).wait_recv()
            shell_copy(s, source, partner, fwd_send.at[e - 1, s]).start()

    def over_x(s, start):
        for e in range(1, nx):
            copy = shell_copy(s, sh, xpeer(e), x_send.at[e - 1, s])
            copy.start() if start else copy.wait_send()

    ahead = planes // 2
    chunk = side // 4

    def mix(source, those, first=False, last=False):
        def rows(i, _):
            c = i * chunk if last else pl.multiple_of(i * chunk, chunk)
            got = [gath[source, s, pl.ds(c, chunk), :].astype(F32) for s in those]
            for j in range(planes):
                total = None if first else acc[j, pl.ds(c, chunk), :]
                for s, plane in zip(those, got):
                    term = table[j, pl.ds(source * planes + s, 1), :] * plane
                    total = term if total is None else total + term
                if last:
                    half[pl.ds(c * planes + j, chunk, stride=planes), :] = total
                else:
                    acc[j, pl.ds(c, chunk), :] = total
            return 0

        if last:
            for i in range(side // chunk):
                rows(i, 0)
        else:
            lax.fori_loop(0, side // chunk, rows, 0)

    landed = stage.at[pl.ds(0, (ntile - 1) * lead)]
    pltpu.make_async_copy(landed, landed, a2a_recv).wait()
    pixels = stage[...]
    if pixels.shape[1] % 16:
        pixels = pixels.astype(F32).reshape(half.shape).astype(BF16)
    half[...] = jnp.dot(pixels.reshape(half.shape), cols_v[...], preferred_element_type=F32)
    for s in range(planes):
        plane = half[pl.ds(s, side, stride=planes), :].astype(BF16)
        gath[sh, s] = jnp.dot(filt, plane, preferred_element_type=F32).astype(BF16)
        if s < ahead:
            over_x(s, True)
        shell_copy(s, sh, partner, near_send.at[s]).start()
    for s in range(ahead, planes):
        over_x(s - ahead, False)
        over_x(s, True)
        if s == ahead:
            mix(sh, list(range(planes)), first=True)
    for s in range(planes):
        shell_copy(s, partner, sh, near_send.at[s]).wait_recv()
    mix(partner, list(range(planes)))
    for s in range(planes):
        forward(s)
    for e in range(1, nx):
        mix(xpeer(nx - e), list(range(planes)))
    for e in range(1, nx):
        source = lax.rem(xi + nx - e, nx) * CORES + (1 - core)
        for s in range(0, planes, ahead):
            those = list(range(s, s + ahead))
            for t in those:
                shell_copy(t, source, sh, fwd_send.at[e - 1, t]).wait_recv()
            mix(source, those, last=e == nx - 1 and s == planes - ahead)
    out[...] = half[...].astype(BF16).reshape(out.shape)

    gone = rays.at[pl.ds(0, (ntile - 1) * lead)]
    pltpu.make_async_copy(gone, gone, a2a_send).wait()
    for s in range(planes):
        shell_copy(s, sh, partner, near_send.at[s]).wait_send()
        if s >= planes - ahead:
            over_x(s, False)
        for e in range(1, nx):
            shell_copy(s, xpeer(nx - e), partner, fwd_send.at[e - 1, s]).wait_send()


def shards(residual, tile_ray, filter_rows, filter_cols, band_lo, shell_weight):
    planes, rays = residual.shape
    nshell, ntile = lax.axis_size("shell"), lax.axis_size("tile")
    side = filter_rows.shape[0]
    count = band_lo.shape[0]
    nx = nshell // CORES
    blk = side // ntile
    fold = 4 if blk % 4 == 0 else 1
    major, group = side // fold, planes * fold
    arranged = residual.reshape(planes, side, side).transpose(1, 0, 2).reshape(major, group, side)
    operands = (arranged, tile_ray.reshape(1, side), filter_rows, filter_cols, band_lo, shell_weight)
    dma = pltpu.SemaphoreType.DMA
    result = pl.pallas_call(
        functools.partial(body, nshell, ntile, planes),
        out_shape=jax.ShapeDtypeStruct((major, group, side), BF16),
        in_specs=[pl.BlockSpec(memory_space=pltpu.HBM)] * 6,
        out_specs=pl.BlockSpec(memory_space=pltpu.VMEM),
        scratch_shapes=[
            pltpu.VMEM((major, group, side), BF16),
            pltpu.VMEM((nshell, planes, side, side), BF16),
            pltpu.VMEM((side * planes, side), F32),
            pltpu.VMEM((planes, side, side), F32),
            pltpu.VMEM((1, side), jnp.int32),
            pltpu.VMEM((side, side), BF16),
            pltpu.VMEM((side, side), BF16),
            pltpu.SMEM((count,), jnp.int32),
            pltpu.SMEM((count,), F32),
            pltpu.VMEM((planes, count, side), F32),
            dma((6,)),
            dma,
            dma,
            dma((nx - 1, planes)),
            dma((planes,)),
            dma((nx - 1, planes)),
            dma((nshell, planes)),
        ],
        compiler_params=pltpu.CompilerParams(
            collective_id=0, has_side_effects=True, vmem_limit_bytes=16 * 1024 * 1024
        ),
    )(*(pltpu.with_memory_space_constraint(x, pltpu.HBM) for x in operands))
    return result.reshape(side, planes, side).transpose(1, 0, 2).reshape(planes, rays)


def solution(mesh):
    in_specs = (P("shell", "tile"), P("tile"), P(), P(), P(), P())
    out_specs = P("shell", "tile")
    return jax.shard_map(shards, mesh=mesh, in_specs=in_specs, out_specs=out_specs, check_vma=False)
```
